256 devices in a mesh: case: 4 (over y), se: 64 (over x, z, core).
Axes of the slice: x: 4, y: 4, z: 8, core: 2. Of those that a mesh axis runs over, the one named last changes fastest.
Arguments:
- panel_press: bfloat16 [131072, 512], P('se', 'case'), may hold values from -1.5 to 1.5
- panel_owner: int32 [131072, 1], P('se'), may hold values from 0 to 63; in each aligned block of 2048 rows (0 to 2047, 2048 to 4095, ...) at most 64 rows name the same one
- panel_slot: int32 [131072], P('se'), may hold values from 0 to 511
- elem_count: int32 [64], P('se'), may hold values from 1024 to 4096
- flexibility: bfloat16 [64, 2560, 512], P('se'), may hold values from -0.25 to 0.25
- stress_matrix: bfloat16 [64, 4096, 2560], P('se', 'case'), may hold values from -0.125 to 0.125
- combination: bfloat16 [512, 256], replicated, may hold values from -0.25 to 0.25
Outputs:
- combined: bfloat16 [64, 4096, 256], P('se', 'case')
The draws below stay inside these ranges and needn't reach their ends.
Inputs may be any that keep to these rules, and one draw needn't show every extreme that they name: `panel_owner`: of the 2048 panels of one index of se, at most 64 name one superelement, a bound that some block reaches of them.
All inputs are finite; a program needn't handle non-finite values.
Results may differ from the reference program's by a relative error of at most 0.0064.
Values may be sent and summed in bfloat16 or wider, within the bound.
No kernel may reach another device: no remote copies, remote signals or barrier semaphores. Data moves between devices by JAX's collectives and lax.ppermute only.
A program may use at most 128 MiB of HBM per device.

```python
import math
import jax
import jax.numpy as jnp
import numpy as np
from jax import lax

NLOAD = 512
NDOF = 2560
ELEM = 4096
COMBOS = 256
PAN_DEV = 2048
CASES = 512
SES = 64
PANELS = 131072
CAP = 64
N_SE = 64


def with_ends(drawn, key, smallest, largest):
    dims = drawn.shape
    place = [jax.random.randint(jax.random.fold_in(key, axis), (), 0, dims[axis]) for axis in range(len(dims))]
    drawn = drawn.at[tuple(place)].set(smallest)
    longest = dims.index(max(dims))
    place[longest] = (place[longest] + 1) % dims[longest]
    return drawn.at[tuple(place)].set(largest)


def level_of(own_key, shape, pieces, least, top_value):
    level, own = 1.0, jax.random.fold_in(own_key, 6)
    for dim, shards_of in pieces:
        heights = jnp.exp(jax.random.uniform(jax.random.fold_in(own, dim), (shards_of,), jnp.float32, least / len(pieces), top_value / len(pieces)))
        level = level * jnp.repeat(heights, shape[dim] // shards_of).reshape([-1 if axis == dim else 1 for axis in range(len(shape))])
    return level


def shared_out(key, own, number, rows, amount, top, reach, slope):
    sequence = jax.random.permutation(key, amount)
    heavy_load, ordinary = portions_of(amount, rows * top, reach, slope, True), portions_of(amount, rows * top, reach, slope, False)
    places = jnp.arange(amount)

    def named(lengths, offset_by):
        used = int((lengths > 0).sum())
        fixed = max(1, used // 4)
        passed = fixed + (places - fixed + offset_by * (used - fixed)) % max(1, amount - fixed)
        return jnp.zeros((amount,), jnp.int32).at[sequence[jnp.where(places < fixed, places, passed)]].set(jnp.asarray(lengths, jnp.int32))

    lengths = jnp.where(number % 4 == 0, named(heavy_load, number // 4), named(ordinary, number - number // 4 - 1))
    mixed = jax.random.permutation(jax.random.fold_in(own, 3), amount)
    giver, taker = mixed[0:amount // 2 * 2:2], mixed[1:amount // 2 * 2:2]
    room = jnp.minimum(lengths[giver] - 1, reach - lengths[taker]) // 2
    room = jnp.where((giver == sequence[0]) | (taker == sequence[0]) | (lengths[taker] == 0), 0, jnp.maximum(room, 0))
    passed = jax.random.randint(jax.random.fold_in(own, 4), (amount // 2,), 0, 1 << 20) % (room + 1)
    lengths = lengths.at[giver].add(-passed).at[taker].add(passed)
    members = jnp.searchsorted(jnp.cumsum(lengths), jnp.arange(rows * top), side="right").astype(jnp.int32)
    listing = members.reshape(top, rows).T
    listing = listing[jax.random.permutation(jax.random.fold_in(own, 1), rows)]
    offset_by = jax.random.randint(jax.random.fold_in(own, 2), (rows, 1), 0, top)
    return jnp.take_along_axis(listing, (jnp.arange(top)[None, :] + offset_by) % top, axis=1)


def portions_of(amount, total, bound, lean, full):
    portions = [(1 << 20) // math.isqrt(rank ** lean) + 1 for rank in range(1, amount + 1)]
    largest = bound if full else min(bound, max(-(-total // amount), total * portions[0] // sum(portions)))
    least = 1 if total - largest >= amount - 1 else 0
    holding, surplus = [largest] + [least] * (amount - 1), total - largest - least * (amount - 1)
    while surplus > 0:
        movable = [i for i in range(1, amount) if holding[i] < largest] or [i for i in range(1, amount) if holding[i] < bound]
        pool, left = sum([portions[i] for i in movable]), surplus
        for i in movable:
            more = min(bound - holding[i], max(1, left * portions[i] // pool), surplus)
            holding[i] = holding[i] + more
            surplus = surplus - more
    return np.array(holding)


def centred(own_key, shape, width, reach, cuts=(), kind=jnp.bfloat16):
    values = jax.random.normal(own_key, shape, jnp.float32) * width
    if len(cuts) > 0:
        values = level_of(own_key, shape, cuts, -0.22, 0.18) * values
    return jnp.clip(values, min=-reach, max=reach).astype(kind)


def setup_inputs(seed: int = 0) -> dict:
    splits = jax.random.split(jax.random.key(seed), 8)
    panel_press = centred(splits[0], (PANELS, CASES), 0.25, 1.5, ((0, 64), (1, 4)))
    panel_owner_keys = jax.random.split(jax.random.fold_in(splits[1], 1), PANELS // PAN_DEV)
    panel_owner_turns = jax.random.permutation(jax.random.fold_in(splits[1], 3), PANELS // PAN_DEV)
    panel_owner = jax.vmap(lambda own, number: shared_out(jax.random.fold_in(splits[1], 2), own, number, PAN_DEV, N_SE, 1, CAP, 2))(panel_owner_keys, panel_owner_turns).reshape((PANELS, 1))
    panel_slot = with_ends(jax.random.randint(splits[2], (PANELS,), 0, NLOAD), jax.random.fold_in(splits[2], 1), 0, NLOAD - 1).astype(jnp.int32)
    elem_count = with_ends(jax.random.randint(splits[3], (SES,), ELEM // 4, ELEM + 1), jax.random.fold_in(splits[3], 1), ELEM // 4, ELEM).astype(jnp.int32)
    flexibility = centred(splits[4], (SES, NDOF, NLOAD), NLOAD ** -0.5, 0.25, ((0, 64),))
    stress_matrix = centred(splits[5], (SES, ELEM, NDOF), NDOF ** -0.5, 0.125, ((0, 64), (1, 4)))
    combination = centred(splits[6], (CASES, COMBOS), CASES ** -0.5, 0.25)
    return {"panel_press": panel_press, "panel_owner": panel_owner, "panel_slot": panel_slot, "elem_count": elem_count, "flexibility": flexibility, "stress_matrix": stress_matrix, "combination": combination}


def reference(panel_press, panel_owner, panel_slot, elem_count, flexibility, stress_matrix, combination):
    segment_ids = panel_owner[:, 0] * NLOAD + panel_slot
    load_sums = jax.ops.segment_sum(panel_press.astype(jnp.float32), segment_ids, num_segments=SES * NLOAD)
    loads = load_sums.astype(jnp.bfloat16).reshape(SES, NLOAD, CASES)
    row_ids = jnp.arange(ELEM, dtype=jnp.int32)

    def recover(items):
        flex_one, load_one, stress_one, live_rows = items
        displacement = jnp.dot(flex_one, load_one, preferred_element_type=jnp.float32).astype(jnp.bfloat16)
        stress = jnp.dot(stress_one, displacement, preferred_element_type=jnp.float32)
        stress = jnp.where(row_ids[:, None] < live_rows, stress, 0.0).astype(jnp.bfloat16)
        return jnp.dot(stress, combination, preferred_element_type=jnp.float32).astype(jnp.bfloat16)

    return lax.map(recover, (flexibility, loads, stress_matrix, elem_count))
```

```python
import jax
import jax.numpy as jnp
from jax import lax
from jax.experimental import pallas as pl
from jax.experimental.pallas import tpu as pltpu
from jax.sharding import PartitionSpec as P

NX, NZ, NC = 4, 8, 2
CAP = 64
NEAR = NX * NC
ROWS = NEAR * CAP
META = 16
MSG = ROWS + META
BF, F32 = jnp.bfloat16, jnp.float32


def iota(shape, dim):
    return lax.broadcasted_iota(jnp.int32, shape, dim)


def one_hot(mask):
    return jnp.where(mask, 1.0, 0.0).astype(BF)


def pack_kernel(owner_ref, slot_ref, press_ref, out_ref, place_ref, dist_ref, meta_ref):
    step = pl.program_id(0)
    panels = press_ref.shape[0]

    @pl.when(step == 0)
    def _():
        me = lax.axis_index("se")
        owner = owner_ref[...]
        dx = ((owner >> 4) - (me >> 4)) & (NX - 1)
        dz = ((owner >> 1) - (me >> 1)) & (NZ - 1)
        dc = (owner ^ me) & 1
        near = dc * NX + dx
        q = dz * NEAR + near
        oh_q = one_hot(iota((NZ * NEAR, panels), 0) == q)
        width = 256
        before = one_hot(iota((width, width), 0) < iota((width, width), 1))
        blocks = one_hot((iota((panels, 128), 0) // width) < iota((panels, 128), 1))
        starts = jnp.dot(oh_q, blocks, preferred_element_type=F32)
        ranks = []
        for b in range(panels // width):
            part = oh_q[:, b * width : (b + 1) * width]
            count = jnp.dot(part, before, preferred_element_type=F32) + starts[:, b : b + 1]
            ranks.append(jnp.sum(part.astype(F32) * count, axis=0, keepdims=True))
        rank = jnp.concatenate(ranks, axis=1).astype(jnp.int32)
        place_ref[...] = one_hot(iota((ROWS, panels), 0) == near * CAP + rank)
        dist_ref[...] = jnp.where(iota((NZ, panels), 0) == dz, 1.0, 0.0)
        row = iota((NZ * META, panels), 0)
        hit = ((row >> 4) == dz) & ((row & 15) == (near >> 1))
        value = (slot_ref[...] - 256).astype(F32)
        rows_at = jnp.where(hit, value, 0.0).astype(BF)
        lanes_at = one_hot(iota((128, panels), 0) == (near & 1) * CAP + rank)
        meta_ref[...] = lax.dot_general(
            rows_at, lanes_at, (((1,), (1,)), ((), ())), preferred_element_type=F32
        ).astype(BF)

    chosen = place_ref[...] * dist_ref[pl.ds(step, 1), :].astype(BF)
    out_ref[0, :ROWS, :] = jnp.dot(chosen, press_ref[...], preferred_element_type=F32).astype(BF)
    out_ref[0, ROWS:, :] = meta_ref[pl.ds(pl.multiple_of(step * META, META), META), :]


def pack(owner, slot, press):
    panels, cases = press.shape
    return pl.pallas_call(
        pack_kernel,
        grid=(NZ,),
        in_specs=[
            pl.BlockSpec((1, panels), lambda i: (0, 0)),
            pl.BlockSpec((1, panels), lambda i: (0, 0)),
            pl.BlockSpec((panels, cases), lambda i: (0, 0)),
        ],
        out_specs=pl.BlockSpec((1, MSG, cases), lambda i: (i, 0, 0)),
        out_shape=jax.ShapeDtypeStruct((NZ, MSG, cases), BF),
        scratch_shapes=[
            pltpu.VMEM((ROWS, panels), BF),
            pltpu.VMEM((NZ, panels), F32),
            pltpu.VMEM((NZ * META, 128), BF),
        ],
        compiler_params=pltpu.CompilerParams(vmem_limit_bytes=32 << 20),
        cost_estimate=pl.CostEstimate(
            flops=2 * NZ * ROWS * panels * cases, bytes_accessed=2 << 20, transcendentals=0
        ),
        name="pack",
    )(owner, slot, press)


def scatter_kernel(*refs):
    msgs, (own_ref, mate_ref) = refs[:NZ], refs[NZ:]
    points = own_ref.shape[1]
    lane = iota((1, 128), 1)
    point = iota((points, 128), 0)
    for near in range(NEAR):
        row = near // 2
        ohs, data = [], []
        for m in range(0, NZ, 2):
            first = msgs[m][ROWS : ROWS + META, :].astype(F32)[row : row + 1, :]
            second = msgs[m + 1][ROWS : ROWS + META, :].astype(F32)[row : row + 1, :]
            if near % 2 == 0:
                second = pltpu.roll(second, CAP, 1)
            else:
                first = pltpu.roll(first, CAP, 1)
            slots = jnp.where(lane < CAP, first, second).astype(jnp.int32) + 256
            ohs.append(one_hot(point == slots))
            data.append(msgs[m][near * CAP : (near + 1) * CAP, :])
            data.append(msgs[m + 1][near * CAP : (near + 1) * CAP, :])
        total = jnp.dot(
            jnp.concatenate(ohs, axis=1),
            jnp.concatenate(data, axis=0),
            preferred_element_type=F32,
        ).astype(BF)
        target = own_ref if near < NX else mate_ref
        target[near % NX] = total


def scatter(messages, points):
    cases = messages[0].shape[1]
    shape = jax.ShapeDtypeStruct((NX, points, cases), BF)
    return pl.pallas_call(
        scatter_kernel,
        out_shape=(shape, shape),
        compiler_params=pltpu.CompilerParams(vmem_limit_bytes=32 << 20),
        cost_estimate=pl.CostEstimate(
            flops=2 * NEAR * points * ROWS * cases, bytes_accessed=4 << 20, transcendentals=0
        ),
        name="scatter",
    )(*messages)


def finish_kernel(live_ref, *refs):
    loads, (comb_ref, mat_ref, out_ref) = refs[:NX], refs[NX:]
    y = lax.axis_index("case")
    cases = loads[0].shape[1]
    total = None
    for k in range(len(loads)):
        block = pl.multiple_of(((y - k) & 3) * cases, cases)
        term = jnp.dot(loads[k][...], comb_ref[pl.ds(block, cases), :], preferred_element_type=F32)
        total = term if total is None else total + term
    rows = out_ref.shape[0]
    out = jnp.dot(mat_ref[...], total.astype(BF), preferred_element_type=F32)
    live = y * rows + iota(out.shape, 0) < live_ref[0]
    out_ref[...] = jnp.where(live, out, 0.0).astype(BF)


def finish(live, loads, comb, mat):
    vmem = pl.BlockSpec(memory_space=pltpu.VMEM)
    return pl.pallas_call(
        finish_kernel,
        in_specs=[pl.BlockSpec(memory_space=pltpu.SMEM)] + [vmem] * (len(loads) + 2),
        out_specs=vmem,
        out_shape=jax.ShapeDtypeStruct((mat.shape[0], comb.shape[1]), BF),
        compiler_params=pltpu.CompilerParams(vmem_limit_bytes=32 << 20),
        cost_estimate=pl.CostEstimate(flops=400 << 20, bytes_accessed=3 << 20, transcendentals=0),
        name="finish",
    )(live, *loads, comb, mat)


def se_index(x, z, c):
    return ((x % NX) * NZ + z % NZ) * NC + c % NC


def moved(dx, dz, dc):
    return [
        (se_index(x, z, c), se_index(x + dx, z + dz, c + dc))
        for x in range(NX)
        for z in range(NZ)
        for c in range(NC)
    ]


def per_device(
    panel_press, panel_owner, panel_slot, elem_count, flexibility, stress_matrix, combination
):
    panels = panel_press.shape[0]
    points = flexibility.shape[2]
    packed = pack(
        panel_owner.reshape(1, panels), panel_slot.reshape(1, panels), panel_press
    )
    messages = [packed[0]] + [None] * (NZ - 1)
    for k in (4, 3, 5, 2, 6, 1, 7):
        messages[k] = lax.ppermute(packed[k], "se", moved(0, k, 0))
    mat = jnp.dot(
        stress_matrix[0], flexibility[0], preferred_element_type=F32
    ).astype(BF)
    own, mate = scatter(messages, points)
    mate = lax.ppermute(mate, "se", moved(0, 0, 1))
    sums = (own.astype(F32) + mate.astype(F32)).astype(BF)
    total = sums[0].astype(F32)
    for k in (2, 1, 3):
        total = total + lax.ppermute(sums[k], "se", moved(k, 0, 0)).astype(F32)
    loads = [total.astype(BF)] + [None] * (NX - 1)
    for k in (2, 1, 3):
        loads[k] = lax.ppermute(loads[0], "case", [(y, (y + k) % 4) for y in range(4)])
    return finish(elem_count, loads, combination, mat)[None]


def solution(mesh):
    return jax.shard_map(
        per_device,
        mesh=mesh,
        in_specs=(
            P("se", "case"),
            P("se", None),
            P("se"),
            P("se"),
            P("se", None, None),
            P("se", "case", None),
            P(),
        ),
        out_specs=P("se", "case", None),
        check_vma=False,
    )
```

```python
import functools

import jax
import jax.numpy as jnp
from jax import lax
from jax.experimental import pallas as pl
from jax.experimental.pallas import tpu as pltpu
from jax.sharding import PartitionSpec as P

NX, NZ, NC = 4, 8, 2
CAP = 64
BLOCK = NZ * CAP
CHIPS = NX * NZ
MSG = NC * CAP + 8
BF, F32 = jnp.bfloat16, jnp.float32


def iota(shape, dim):
    return lax.broadcasted_iota(jnp.int32, shape, dim)


def one_hot(mask):
    return jnp.where(mask, 1.0, 0.0).astype(BF)


def pack_kernel(side, owner_ref, slot_ref, press_ref, out_ref):
    panels, cases = press_ref.shape
    me = lax.axis_index("se")
    owner = owner_ref[...]
    mine = ((owner ^ me) & 1) == side
    chip = jnp.where(mine, owner >> 1, -1)
    part = jnp.where(mine, owner >> 4, -1)
    near = (owner >> 1) & (NZ - 1)
    oh = jnp.where(iota((CHIPS, panels), 0) == chip, 1.0, 0.0)
    width = 256
    ohs = [oh[:, b * width : (b + 1) * width] for b in range(panels // width)]
    before = one_hot(iota((width, width), 0) < iota((width, width), 1))
    counts = jnp.dot(jnp.concatenate(ohs, axis=0).astype(BF), before, preferred_element_type=F32)
    start, ranks = jnp.zeros((CHIPS, 1), F32), []
    for b, piece in enumerate(ohs):
        count = counts[b * CHIPS : (b + 1) * CHIPS]
        ranks.append(jnp.sum(piece * (count + start), axis=0, keepdims=True))
        start = start + count[:, width - 1 :] + piece[:, width - 1 :]
    rank = jnp.concatenate(ranks, axis=1).astype(jnp.int32)
    place = one_hot(iota((BLOCK, panels), 0) == near * CAP + rank)

    value = (slot_ref[...] - 256).astype(F32)
    out_ref[CHIPS * CAP :, :] = lax.dot_general(
        (oh * value).astype(BF),
        one_hot(iota((128, panels), 0) == side * CAP + rank),
        (((1,), (1,)), ((), ())),
        preferred_element_type=F32,
    ).astype(BF)

    parts = jnp.transpose(jnp.broadcast_to(part.astype(F32), (128, panels)))
    press = press_ref[...]
    for j in range(0, NX, 2):
        both = [press * one_hot(parts == i) for i in (j, j + 1)]
        rows = jnp.dot(place, jnp.concatenate(both, axis=1), preferred_element_type=F32)
        for i in (j, j + 1):
            out_ref[i * BLOCK : (i + 1) * BLOCK, :] = rows[:, (i - j) * cases : (i - j + 1) * cases].astype(BF)


def pack(side, owner, slot, press):
    panels, cases = press.shape
    return pl.pallas_call(
        functools.partial(pack_kernel, side),
        out_shape=jax.ShapeDtypeStruct((CHIPS * CAP + CHIPS, cases), BF),
        compiler_params=pltpu.CompilerParams(vmem_limit_bytes=32 << 20),
        cost_estimate=pl.CostEstimate(
            flops=2 * CHIPS * CAP * panels * cases, bytes_accessed=2 << 20, transcendentals=0
        ),
        name="pack",
    )(owner, slot, press)


def scatter_kernel(msg_ref, out_ref):
    points, cases = out_ref.shape
    point = iota((points, 128), 0) - 256
    ohs, data = [], []
    for j in range(CHIPS):
        slots = msg_ref[j, NC * CAP :, :].astype(F32)[:1, :].astype(jnp.int32)
        ohs.append(one_hot(point == slots))
        data.append(msg_ref[j, : NC * CAP, :])
    out_ref[...] = jnp.dot(
        jnp.concatenate(ohs, axis=1), jnp.concatenate(data, axis=0), preferred_element_type=F32
    ).astype(BF)


def scatter(messages, points):
    cases = messages.shape[2]
    return pl.pallas_call(
        scatter_kernel,
        out_shape=jax.ShapeDtypeStruct((points, cases), BF),
        compiler_params=pltpu.CompilerParams(vmem_limit_bytes=32 << 20),
        cost_estimate=pl.CostEstimate(
            flops=2 * points * CHIPS * NC * CAP * cases, bytes_accessed=2 << 20, transcendentals=0
        ),
        name="scatter",
    )(messages)


def finish_kernel(live_ref, *refs):
    loads, (comb_ref, mat_ref, out_ref) = refs[:NX], refs[NX:]
    y = lax.axis_index("case")
    cases = loads[0].shape[1]
    total = None
    for k in range(len(loads)):
        block = pl.multiple_of(((y - k) & 3) * cases, cases)
        term = jnp.dot(loads[k][...], comb_ref[pl.ds(block, cases), :], preferred_element_type=F32)
        total = term if total is None else total + term
    rows = out_ref.shape[0]
    out = jnp.dot(mat_ref[...], total.astype(BF), preferred_element_type=F32)
    live = y * rows + iota(out.shape, 0) < live_ref[0]
    out_ref[...] = jnp.where(live, out, 0.0).astype(BF)


def finish(live, loads, comb, mat):
    vmem = pl.BlockSpec(memory_space=pltpu.VMEM)
    return pl.pallas_call(
        finish_kernel,
        in_specs=[pl.BlockSpec(memory_space=pltpu.SMEM)] + [vmem] * (len(loads) + 2),
        out_specs=vmem,
        out_shape=jax.ShapeDtypeStruct((mat.shape[0], comb.shape[1]), BF),
        compiler_params=pltpu.CompilerParams(vmem_limit_bytes=32 << 20),
        cost_estimate=pl.CostEstimate(flops=400 << 20, bytes_accessed=3 << 20, transcendentals=0),
        name="finish",
    )(live, *loads, comb, mat)


def se_index(x, z, c):
    return (x * NZ + z) * NC + c


SAME_CORE = [[se_index(x, z, c) for x in range(NX) for z in range(NZ)] for c in range(NC)]
OTHER_CORE = [(i, i ^ 1) for i in range(NX * NZ * NC)]


def per_device(
    panel_press, panel_owner, panel_slot, elem_count, flexibility, stress_matrix, combination
):
    panels, cases = panel_press.shape
    points = flexibility.shape[2]
    owner, slot = panel_owner.reshape(1, panels), panel_slot.reshape(1, panels)
    theirs = lax.ppermute(pack(1, owner, slot, panel_press), "se", OTHER_CORE)
    ours = pack(0, owner, slot, panel_press)
    slots = ours[CHIPS * CAP :] + theirs[CHIPS * CAP :]
    messages = jnp.concatenate(
        [
            ours[: CHIPS * CAP].reshape(CHIPS, CAP, cases),
            theirs[: CHIPS * CAP].reshape(CHIPS, CAP, cases),
            jnp.broadcast_to(slots[:, None, :], (CHIPS, MSG - NC * CAP, cases)),
        ],
        axis=1,
    )
    messages = lax.all_to_all(messages, "se", 0, 0, axis_index_groups=SAME_CORE, tiled=True)
    loads = [scatter(messages, points)]
    for k in (1, 2, 3):
        loads.append(lax.ppermute(loads[0], "case", [(y, (y + k) % 4) for y in range(4)]))
    mat = jnp.dot(
        stress_matrix[0], flexibility[0], preferred_element_type=F32
    ).astype(BF)
    return finish(elem_count, loads, combination, mat)[None]


def solution(mesh):
    return jax.shard_map(
        per_device,
        mesh=mesh,
        in_specs=(
            P("se", "case"),
            P("se", None),
            P("se"),
            P("se"),
            P("se", None, None),
            P("se", "case", None),
            P(),
        ),
        out_specs=P("se", "case", None),
        check_vma=False,
    )
```

```python
import jax
import jax.numpy as jnp
from jax import lax
from jax.experimental import pallas as pl
from jax.experimental.pallas import tpu as pltpu
from jax.sharding import PartitionSpec as P

NX, NZ, NC, NY = 4, 8, 2, 4
CAP = 64
CHIPS = NX * NZ
LANES, HALF = 128, 64
PER = CAP // 2
GROUP = 16
MSG = NC * PER + 8
OUT_PARTS = 4
FETCH_VMEM = 52
BF, F32 = jnp.bfloat16, jnp.float32


def iota(shape, dim):
    return lax.broadcasted_iota(jnp.int32, shape, dim)


def one_hot(mask):
    return jnp.where(mask, 1.0, 0.0).astype(BF)


def dot(a, b):
    return jnp.dot(a, b, preferred_element_type=F32)


def call(kernel, out_shape, args, flops, name, in_specs=None, vmem=32, **more):
    if in_specs is not None:
        more["in_specs"] = in_specs
    return pl.pallas_call(
        kernel,
        out_shape=out_shape,
        compiler_params=pltpu.CompilerParams(vmem_limit_bytes=vmem << 20),
        cost_estimate=pl.CostEstimate(flops=flops, bytes_accessed=2 << 20, transcendentals=0),
        name=name,
        **more,
    )(*args)


def project_kernel(press_hbm, comb_hbm, own_ref, *refs):
    send_refs, (press_ref, comb_ref, sems) = refs[: NY - 1], refs[NY - 1 :]
    panels, cases = press_ref.shape
    combos = comb_ref.shape[1]
    y = lax.axis_index("case")
    at = pl.ds(pl.multiple_of(y * cases, cases), cases)
    comb_copy = pltpu.make_async_copy(comb_hbm.at[at], comb_ref, sems.at[0])
    press_copy = pltpu.make_async_copy(press_hbm, press_ref, sems.at[1])
    comb_copy.start()
    press_copy.start()
    source, target = iota((combos, NY * LANES), 0), iota((combos, NY * LANES), 1)
    lane = target & (LANES - 1)
    turn = 1 - 2 * (lax.axis_index("se") & 1)
    column = ((target >> 7) * (turn * HALF) + (lane & (HALF - 1)) + y * HALF) & (combos - 1)
    left = one_hot((source == column) & (lane < HALF))
    right = one_hot((source == column) & (lane >= HALF))
    comb_copy.wait()
    mine = comb_ref[...]
    first, second = dot(mine, left).astype(BF), dot(mine, right).astype(BF)
    press_copy.wait()
    half = panels // 2
    both = jnp.concatenate([press_ref[:half, :], press_ref[half:, :]], axis=1)
    product = dot(both, jnp.concatenate([first, second], axis=0))
    own_ref[...] = product[:, :LANES]
    for k, ref in enumerate(send_refs):
        ref[...] = product[:, (k + 1) * LANES : (k + 2) * LANES].astype(BF)


def rank_kernel(owner_ref, slot_ref, place_ref, masks_ref, meta_ref):
    panels = owner_ref.shape[1]
    me = lax.axis_index("se")
    owner = owner_ref[...]
    side = (owner ^ me) & 1
    chip = owner >> 1
    owners = CHIPS * NC
    oh = jnp.where(iota((owners, panels), 0) == side * CHIPS + chip, 1.0, 0.0)
    width = 256
    ohs = [oh[:, b * width : (b + 1) * width] for b in range(panels // width)]
    before = one_hot(iota((width, width), 0) < iota((width, width), 1))
    counts = dot(jnp.concatenate(ohs, axis=0).astype(BF), before)
    start, ranks = jnp.zeros((owners, 1), F32), []
    for b, piece in enumerate(ohs):
        count = counts[b * owners : (b + 1) * owners]
        ranks.append(jnp.sum(piece * (count + start), axis=0, keepdims=True))
        start = start + count[:, width - 1 :] + piece[:, width - 1 :]
    rank = jnp.concatenate(ranks, axis=1).astype(jnp.int32)
    low, high = rank & (PER - 1), rank // PER
    place_ref[...] = one_hot(iota((GROUP * PER, panels), 0) == (chip & (GROUP - 1)) * PER + low)
    lanes = high * HALF + side * PER + low
    meta_ref[...] = lax.dot_general(
        (oh * (slot_ref[...] - 256).astype(F32)).astype(BF),
        one_hot(iota((LANES, panels), 0) == lanes),
        (((1,), (1,)), ((), ())),
        preferred_element_type=F32,
    ).astype(BF)
    group = side * 4 + (chip // GROUP) * 2 + high
    groups = jnp.transpose(jnp.broadcast_to(group.astype(F32), (LANES, panels)))
    part = (iota((1, LANES), 1) // HALF).astype(F32)
    for s in range(NC):
        for h in range(2):
            masks_ref[s, :, h * LANES : (h + 1) * LANES] = one_hot(groups == part + (s * 4 + h * 2))


def place_rows(rows, place_ref, mask_ref, meta_ref, out_ref):
    lane = iota(rows.shape, 1)
    turned = pltpu.roll(rows, HALF, 1)
    first = jnp.where(lane < HALF, rows, turned).astype(BF)
    second = jnp.where(lane < HALF, turned, rows).astype(BF)
    each = jnp.concatenate([first, second], axis=0)
    placed = dot(place_ref[...], jnp.concatenate([each, each], axis=1) * mask_ref[0])
    size = GROUP * PER
    for h in range(2):
        out_ref[h * size : (h + 1) * size, :] = placed[:, h * LANES : (h + 1) * LANES].astype(BF)
    out_ref[2 * size :, :] = meta_ref[...]


def sum_and_pack(own_ref, r1_ref, r2_ref, r3_ref, place_ref, mask_ref, meta_ref, out_ref, rows_ref):
    rows = own_ref[...] + r1_ref[...].astype(F32) + r2_ref[...].astype(F32) + r3_ref[...].astype(F32)
    rows_ref[...] = rows
    place_rows(rows, place_ref, mask_ref, meta_ref, out_ref)


def pack_kernel(rows_ref, place_ref, mask_ref, meta_ref, out_ref):
    place_rows(rows_ref[...], place_ref, mask_ref, meta_ref, out_ref)


def pack(kernel, side, rows, place, masks, meta, out_shape):
    whole = [pl.BlockSpec(a.shape, lambda i: (0, 0)) for a in rows]
    return call(
        kernel,
        out_shape,
        (*rows, place, masks, meta),
        1 << 30,
        "pack",
        grid=(1,),
        in_specs=whole
        + [
            pl.BlockSpec(place.shape, lambda i: (0, 0)),
            pl.BlockSpec((1,) + masks.shape[1:], lambda i: (side, 0, 0)),
            pl.BlockSpec((CHIPS, LANES), lambda i: (side, 0)),
        ],
        out_specs=jax.tree.map(lambda s: pl.BlockSpec(s.shape, lambda i: (0, 0)), out_shape),
    )


def scatter_kernel(msg_ref, out_ref):
    points = 2 * out_ref.shape[0]
    point = (iota((points, LANES), 0) - 256).astype(F32).astype(BF)
    left = iota((1, LANES), 1) < HALF
    one, zero = jnp.ones((), BF), jnp.zeros((), BF)
    lows, highs, data = [], [], []
    for j in range(0, CHIPS, 2):
        a, b = (
            msg_ref[i, NC * PER :, :].astype(F32)[:1, :] for i in (j, j + 1)
        )
        low = jnp.where(left, a, pltpu.roll(b, HALF, 1)).astype(BF)
        high = jnp.where(left, pltpu.roll(a, HALF, 1), b).astype(BF)
        lows.append(jnp.where(point == low, one, zero))
        highs.append(jnp.where(point == high, one, zero))
        data += [msg_ref[i, : NC * PER, :] for i in (j, j + 1)]
    rows = jnp.concatenate(data, axis=0)
    total = dot(jnp.concatenate(lows, axis=1), rows)
    total = total + pltpu.roll(dot(jnp.concatenate(highs, axis=1), rows), HALF, 1)
    half = points // 2
    right = pltpu.roll(total[half:], HALF, 1)
    out_ref[...] = jnp.where(left, total[:half], right).astype(BF)


def finish_kernel(live_ref, *refs):
    loads, (mat_ref, out_ref, block_ref, sems) = refs[:NY], refs[NY:]
    y = lax.axis_index("case")
    rows, combos = block_ref.shape
    source, target = iota((NY * LANES, combos), 0), iota((NY * LANES, combos), 1)
    lane = source & (LANES - 1)
    turn = 1 - 2 * (lax.axis_index("se") & 1)
    hit = ((y - turn * (source >> 7)) & (NY - 1)) * HALF + (lane & (HALF - 1)) == target
    every = jnp.concatenate([ref[...] for ref in loads], axis=1)
    upper = dot(every, one_hot(hit & (lane < HALF)))
    lower = dot(every, one_hot(hit & (lane >= HALF)))
    total = jnp.concatenate([upper, lower], axis=0).astype(BF)
    part = rows // OUT_PARTS
    copies = []
    for p in range(OUT_PARTS):
        at = pl.ds(p * part, part)
        out = dot(mat_ref[at, :], total)
        live = y * rows + p * part + iota(out.shape, 0) < live_ref[0]
        block_ref[at, :] = jnp.where(live, out, 0.0).astype(BF)
        copies.append(pltpu.make_async_copy(block_ref.at[at], out_ref.at[at], sems.at[p]))
        copies[-1].start()
    for copy in copies:
        copy.wait()


def se_index(x, z, c):
    return (x * NZ + z) * NC + c


SAME_CORE = [[se_index(x, z, c) for x in range(NX) for z in range(NZ)] for c in range(NC)]
OTHER_CORE = [(i, i ^ 1) for i in range(NX * NZ * NC)]


def along_y(a, k):
    owners = NX * NZ * NC
    pairs = [
        (y * owners + i, (y + (k if i % NC == 0 else -k)) % NY * owners + i)
        for y in range(NY)
        for i in range(owners)
    ]
    return lax.ppermute(a, ("case", "se"), pairs)


def shape(*dims, dtype=BF):
    return jax.ShapeDtypeStruct(dims, dtype)


def per_device(
    panel_press, panel_owner, panel_slot, elem_count, flexibility, stress_matrix, combination
):
    panels = panel_press.shape[0]
    points, combos = flexibility.shape[2], combination.shape[1]
    half = panels // 2
    own, *sent = call(
        project_kernel,
        [shape(half, LANES, dtype=F32)] + [shape(half, LANES)] * (NY - 1),
        (panel_press, combination),
        1 << 28,
        "project",
        in_specs=[pl.BlockSpec(memory_space=pltpu.HBM)] * 2,
        vmem=FETCH_VMEM,
        scratch_shapes=[
            pltpu.VMEM(panel_press.shape, BF),
            pltpu.VMEM((panel_press.shape[1], combos), BF),
            pltpu.SemaphoreType.DMA((2,)),
        ],
    )
    parts = [own] + [along_y(sent[k - 1], k) for k in range(1, NY)]
    place, masks, meta = call(
        rank_kernel,
        (shape(GROUP * PER, panels), shape(NC, panels, 2 * LANES), shape(NC * CHIPS, LANES)),
        (panel_owner.reshape(1, panels), panel_slot.reshape(1, panels)),
        1 << 28,
        "rank",
    )
    mat = dot(stress_matrix[0], flexibility[0]).astype(BF)
    parts, mat = lax.optimization_barrier((parts, mat))
    packed = shape(CHIPS * PER + CHIPS, LANES)
    theirs, rows = pack(
        sum_and_pack, 1, parts, place, masks, meta, (packed, shape(half, LANES, dtype=F32))
    )
    theirs = lax.ppermute(theirs, "se", OTHER_CORE)
    ours = pack(pack_kernel, 0, [rows], place, masks, meta, packed)
    slots = ours[CHIPS * PER :] + theirs[CHIPS * PER :]
    messages = jnp.concatenate(
        [
            ours[: CHIPS * PER].reshape(CHIPS, PER, LANES),
            theirs[: CHIPS * PER].reshape(CHIPS, PER, LANES),
            jnp.broadcast_to(slots[:, None, :], (CHIPS, MSG - NC * PER, LANES)),
        ],
        axis=1,
    )
    messages = lax.all_to_all(messages, "se", 0, 0, axis_index_groups=SAME_CORE, tiled=True)
    loads = [call(scatter_kernel, shape(points // 2, LANES), (messages,), 1 << 30, "scatter")]
    loads += [along_y(loads[0], k) for k in range(1, NY)]
    local = mat.shape[0]
    vmem = pl.BlockSpec(memory_space=pltpu.VMEM)
    out = call(
        finish_kernel,
        shape(local, combos),
        (elem_count, *loads, mat),
        1 << 28,
        "finish",
        in_specs=[pl.BlockSpec(memory_space=pltpu.SMEM)] + [vmem] * (NY + 1),
        out_specs=pl.BlockSpec(memory_space=pltpu.HBM),
        scratch_shapes=[pltpu.VMEM((local, combos), BF), pltpu.SemaphoreType.DMA((OUT_PARTS,))],
    )
    return out[None]


def solution(mesh):
    return jax.shard_map(
        per_device,
        mesh=mesh,
        in_specs=(
            P("se", "case"),
            P("se", None),
            P("se"),
            P("se"),
            P("se", None, None),
            P("se", "case", None),
            P(),
        ),
        out_specs=P("se", "case", None),
        check_vma=False,
    )
```

```python
import jax
import jax.numpy as jnp
from jax import lax
from jax.experimental import pallas as pl
from jax.experimental.pallas import tpu as pltpu
from jax.sharding import PartitionSpec as P

NX, NZ, NC, NY = 4, 8, 2, 4
CAP = 64
CHIPS = NX * NZ
LANES, HALF = 128, 64
PER = CAP // 2
GROUP = 16
MSG = NC * PER + 8
OUT_PARTS = 4
FETCH_VMEM = 53
BF, F32 = jnp.bfloat16, jnp.float32


def iota(shape, dim):
    return lax.broadcasted_iota(jnp.int32, shape, dim)


def one_hot(mask):
    return jnp.where(mask, 1.0, 0.0).astype(BF)


def dot(a, b):
    return jnp.dot(a, b, preferred_element_type=F32)


def call(kernel, out_shape, args, flops, name, in_specs=None, vmem=32, **more):
    if in_specs is not None:
        more["in_specs"] = in_specs
    return pl.pallas_call(
        kernel,
        out_shape=out_shape,
        compiler_params=pltpu.CompilerParams(vmem_limit_bytes=vmem << 20),
        cost_estimate=pl.CostEstimate(flops=flops, bytes_accessed=2 << 20, transcendentals=0),
        name=name,
        **more,
    )(*args)


def pieces(first, count, combos):
    turn = 1 - 2 * (lax.axis_index("se") & 1)
    source, target = iota((combos, count * LANES), 0), iota((combos, count * LANES), 1)
    lane = target & (LANES - 1)
    y = lax.axis_index("case") + turn * ((target >> 7) + first)
    hit = source == ((y * HALF + (lane & (HALF - 1))) & (combos - 1))
    return one_hot(hit & (lane < HALF)), one_hot(hit & (lane >= HALF))


def product(press, comb, picked):
    half = press.shape[0] // 2
    both = jnp.concatenate([press[:half], press[half:]], axis=1)
    return dot(both, jnp.concatenate([dot(comb, p).astype(BF) for p in picked], axis=0))


def case_rows(cases):
    return pl.ds(pl.multiple_of(lax.axis_index("case") * cases, cases), cases)


def project_kernel(press_hbm, comb_hbm, *refs):
    send_refs, (press_ref, comb_ref, sems) = refs[: NY - 1], refs[NY - 1 :]
    comb_copy = pltpu.make_async_copy(
        comb_hbm.at[case_rows(press_ref.shape[1])], comb_ref, sems.at[0]
    )
    press_copy = pltpu.make_async_copy(press_hbm, press_ref, sems.at[1])
    comb_copy.start()
    press_copy.start()
    picked = pieces(1, NY - 1, comb_ref.shape[1])
    comb_copy.wait()
    press_copy.wait()
    sent = product(press_ref[...], comb_ref[...], picked)
    for k, ref in enumerate(send_refs):
        ref[...] = sent[:, k * LANES : (k + 1) * LANES].astype(BF)


def rank_kernel(owner_ref, slot_ref, press_ref, comb_ref, place_ref, masks_ref, meta_ref, own_ref):
    panels = owner_ref.shape[1]
    me = lax.axis_index("se")
    owner = owner_ref[...]
    side = (owner ^ me) & 1
    chip = place_of(owner >> 1, owner & 1)
    owners = CHIPS * NC
    oh = jnp.where(iota((owners, panels), 0) == side * CHIPS + chip, 1.0, 0.0)
    width = 256
    ohs = [oh[:, b * width : (b + 1) * width] for b in range(panels // width)]
    before = one_hot(iota((width, width), 0) < iota((width, width), 1))
    counts = dot(jnp.concatenate(ohs, axis=0).astype(BF), before)
    start, ranks = jnp.zeros((owners, 1), F32), []
    for b, piece in enumerate(ohs):
        count = counts[b * owners : (b + 1) * owners]
        ranks.append(jnp.sum(piece * (count + start), axis=0, keepdims=True))
        start = start + count[:, width - 1 :] + piece[:, width - 1 :]
    rank = jnp.concatenate(ranks, axis=1).astype(jnp.int32)
    low, high = rank & (PER - 1), rank // PER
    place_ref[...] = one_hot(iota((GROUP * PER, panels), 0) == (chip & (GROUP - 1)) * PER + low)
    lanes = high * HALF + side * PER + low
    meta_ref[...] = lax.dot_general(
        (oh * (slot_ref[...] - 256).astype(F32)).astype(BF),
        one_hot(iota((LANES, panels), 0) == lanes),
        (((1,), (1,)), ((), ())),
        preferred_element_type=F32,
    ).astype(BF)
    group = side * 4 + (chip // GROUP) * 2 + high
    groups = jnp.transpose(jnp.broadcast_to(group.astype(F32), (LANES, panels)))
    part = (iota((1, LANES), 1) // HALF).astype(F32)
    for s in range(NC):
        for h in range(2):
            masks_ref[s, :, h * LANES : (h + 1) * LANES] = one_hot(groups == part + (s * 4 + h * 2))
    comb = comb_ref[case_rows(press_ref.shape[1]), :]
    own_ref[...] = product(press_ref[...], comb, pieces(0, 1, comb.shape[1]))


def place_rows(rows, place_ref, mask_ref, meta_ref, out_ref):
    lane = iota(rows.shape, 1)
    turned = pltpu.roll(rows, HALF, 1)
    first = jnp.where(lane < HALF, rows, turned).astype(BF)
    second = jnp.where(lane < HALF, turned, rows).astype(BF)
    each = jnp.concatenate([first, second], axis=0)
    placed = dot(place_ref[...], jnp.concatenate([each, each], axis=1) * mask_ref[0])
    size = GROUP * PER
    for h in range(2):
        out_ref[h * size : (h + 1) * size, :] = placed[:, h * LANES : (h + 1) * LANES].astype(BF)
    out_ref[2 * size :, :] = meta_ref[...]


def sum_and_pack(own_ref, r1_ref, r2_ref, r3_ref, place_ref, mask_ref, meta_ref, out_ref, rows_ref):
    rows = own_ref[...] + r1_ref[...].astype(F32) + r2_ref[...].astype(F32) + r3_ref[...].astype(F32)
    rows_ref[...] = rows
    place_rows(rows, place_ref, mask_ref, meta_ref, out_ref)


def pack_kernel(rows_ref, place_ref, mask_ref, meta_ref, out_ref):
    place_rows(rows_ref[...], place_ref, mask_ref, meta_ref, out_ref)


def pack(kernel, side, rows, place, masks, meta, out_shape):
    whole = [pl.BlockSpec(a.shape, lambda i: (0, 0)) for a in rows]
    return call(
        kernel,
        out_shape,
        (*rows, place, masks, meta),
        1 << 30,
        "pack",
        grid=(1,),
        in_specs=whole
        + [
            pl.BlockSpec(place.shape, lambda i: (0, 0)),
            pl.BlockSpec((1,) + masks.shape[1:], lambda i: (side, 0, 0)),
            pl.BlockSpec((CHIPS, LANES), lambda i: (side, 0)),
        ],
        out_specs=jax.tree.map(lambda s: pl.BlockSpec(s.shape, lambda i: (0, 0)), out_shape),
    )


def scatter_kernel(msg_ref, out_ref):
    points = 2 * out_ref.shape[0]
    point = (iota((points, LANES), 0) - 256).astype(F32).astype(BF)
    left = iota((1, LANES), 1) < HALF
    one, zero = jnp.ones((), BF), jnp.zeros((), BF)
    lows, highs, data = [], [], []
    for j in range(0, CHIPS, 2):
        a, b = (
            msg_ref[i, NC * PER :, :].astype(F32)[:1, :] for i in (j, j + 1)
        )
        low = jnp.where(left, a, pltpu.roll(b, HALF, 1)).astype(BF)
        high = jnp.where(left, pltpu.roll(a, HALF, 1), b).astype(BF)
        lows.append(jnp.where(point == low, one, zero))
        highs.append(jnp.where(point == high, one, zero))
        data += [msg_ref[i, : NC * PER, :] for i in (j, j + 1)]
    rows = jnp.concatenate(data, axis=0)
    total = dot(jnp.concatenate(lows, axis=1), rows)
    total = total + pltpu.roll(dot(jnp.concatenate(highs, axis=1), rows), HALF, 1)
    half = points // 2
    right = pltpu.roll(total[half:], HALF, 1)
    out_ref[...] = jnp.where(left, total[:half], right).astype(BF)


def finish_kernel(live_ref, *refs):
    loads, (mat_ref, out_ref, block_ref, sems) = refs[:NY], refs[NY:]
    y = lax.axis_index("case")
    rows, combos = block_ref.shape
    source, target = iota((NY * LANES, combos), 0), iota((NY * LANES, combos), 1)
    lane = source & (LANES - 1)
    turn = 1 - 2 * (lax.axis_index("se") & 1)
    hit = ((y - turn * (source >> 7)) & (NY - 1)) * HALF + (lane & (HALF - 1)) == target
    every = jnp.concatenate([ref[...] for ref in loads], axis=1)
    upper = dot(every, one_hot(hit & (lane < HALF)))
    lower = dot(every, one_hot(hit & (lane >= HALF)))
    total = jnp.concatenate([upper, lower], axis=0).astype(BF)
    part = rows // OUT_PARTS
    copies = []
    for p in range(OUT_PARTS):
        at = pl.ds(p * part, part)
        out = dot(mat_ref[at, :], total)
        live = y * rows + p * part + iota(out.shape, 0) < live_ref[0]
        block_ref[at, :] = jnp.where(live, out, 0.0).astype(BF)
        copies.append(pltpu.make_async_copy(block_ref.at[at], out_ref.at[at], sems.at[p]))
        copies[-1].start()
    for copy in copies:
        copy.wait()


STRIDE, INVERSE = 7, 23


def place_of(chip, core):
    return (chip * INVERSE + core * (CHIPS // 2)) & (CHIPS - 1)


SAME_CORE = [
    [(place + CHIPS // 2 * c) * STRIDE % CHIPS * NC + c for place in range(CHIPS)] for c in range(NC)
]
OTHER_CORE = [(i, i ^ 1) for i in range(NX * NZ * NC)]


def along_y(a, k):
    owners = NX * NZ * NC
    pairs = [
        (y * owners + i, (y + (k if i % NC == 0 else -k)) % NY * owners + i)
        for y in range(NY)
        for i in range(owners)
    ]
    return lax.ppermute(a, ("case", "se"), pairs)


def shape(*dims, dtype=BF):
    return jax.ShapeDtypeStruct(dims, dtype)


def per_device(
    panel_press, panel_owner, panel_slot, elem_count, flexibility, stress_matrix, combination
):
    panels = panel_press.shape[0]
    points, combos = flexibility.shape[2], combination.shape[1]
    half = panels // 2
    sent = call(
        project_kernel,
        [shape(half, LANES)] * (NY - 1),
        (panel_press, combination),
        1 << 28,
        "project",
        in_specs=[pl.BlockSpec(memory_space=pltpu.HBM)] * 2,
        vmem=FETCH_VMEM,
        scratch_shapes=[
            pltpu.VMEM(panel_press.shape, BF),
            pltpu.VMEM((panel_press.shape[1], combos), BF),
            pltpu.SemaphoreType.DMA((2,)),
        ],
    )
    parts = [along_y(sent[k - 1], k) for k in range(1, NY)]
    place, masks, meta, own = call(
        rank_kernel,
        (
            shape(GROUP * PER, panels),
            shape(NC, panels, 2 * LANES),
            shape(NC * CHIPS, LANES),
            shape(half, LANES, dtype=F32),
        ),
        (panel_owner.reshape(1, panels), panel_slot.reshape(1, panels), panel_press, combination),
        1 << 28,
        "rank",
    )
    mat = dot(stress_matrix[0], flexibility[0]).astype(BF)
    parts, mat = lax.optimization_barrier((parts, mat))
    packed = shape(CHIPS * PER + CHIPS, LANES)
    theirs, rows = pack(
        sum_and_pack, 1, [own, *parts], place, masks, meta, (packed, shape(half, LANES, dtype=F32))
    )
    theirs = lax.ppermute(theirs, "se", OTHER_CORE)
    ours = pack(pack_kernel, 0, [rows], place, masks, meta, packed)
    slots = ours[CHIPS * PER :] + theirs[CHIPS * PER :]
    messages = jnp.concatenate(
        [
            ours[: CHIPS * PER].reshape(CHIPS, PER, LANES),
            theirs[: CHIPS * PER].reshape(CHIPS, PER, LANES),
            jnp.broadcast_to(slots[:, None, :], (CHIPS, MSG - NC * PER, LANES)),
        ],
        axis=1,
    )
    messages = lax.all_to_all(messages, "se", 0, 0, axis_index_groups=SAME_CORE, tiled=True)
    loads = [call(scatter_kernel, shape(points // 2, LANES), (messages,), 1 << 30, "scatter")]
    loads += [along_y(loads[0], k) for k in range(1, NY)]
    local = mat.shape[0]
    vmem = pl.BlockSpec(memory_space=pltpu.VMEM)
    out = call(
        finish_kernel,
        shape(local, combos),
        (elem_count, *loads, mat),
        1 << 28,
        "finish",
        in_specs=[pl.BlockSpec(memory_space=pltpu.SMEM)] + [vmem] * (NY + 1),
        out_specs=pl.BlockSpec(memory_space=pltpu.HBM),
        scratch_shapes=[pltpu.VMEM((local, combos), BF), pltpu.SemaphoreType.DMA((OUT_PARTS,))],
    )
    return out[None]


def solution(mesh):
    return jax.shard_map(
        per_device,
        mesh=mesh,
        in_specs=(
            P("se", "case"),
            P("se", None),
            P("se"),
            P("se"),
            P("se", None, None),
            P("se", "case", None),
            P(),
        ),
        out_specs=P("se", "case", None),
        check_vma=False,
    )
```

```python
import jax
import jax.numpy as jnp
from jax import lax
from jax.experimental import pallas as pl
from jax.experimental.pallas import tpu as pltpu
from jax.sharding import PartitionSpec as P

NX, NZ, NC, NY = 4, 8, 2, 4
CAP = 64
CHIPS = NX * NZ
LANES, HALF = 128, 64
PER = CAP // 2
GROUP = 16
MSG = NC * PER + 8
OUT_PARTS = 4
FETCHES = 8
FETCH_VMEM = 53
BF, F32 = jnp.bfloat16, jnp.float32


def iota(shape, dim):
    return lax.broadcasted_iota(jnp.int32, shape, dim)


def one_hot(mask):
    return jnp.where(mask, 1.0, 0.0).astype(BF)


def dot(a, b):
    return jnp.dot(a, b, preferred_element_type=F32)


def call(kernel, out_shape, args, flops, name, in_specs=None, vmem=32, **more):
    if in_specs is not None:
        more["in_specs"] = in_specs
    return pl.pallas_call(
        kernel,
        out_shape=out_shape,
        compiler_params=pltpu.CompilerParams(vmem_limit_bytes=vmem << 20),
        cost_estimate=pl.CostEstimate(flops=flops, bytes_accessed=2 << 20, transcendentals=0),
        name=name,
        **more,
    )(*args)


def pieces(first, count, combos):
    turn = 1 - 2 * (lax.axis_index("se") & 1)
    source, target = iota((combos, count * LANES), 0), iota((combos, count * LANES), 1)
    lane = target & (LANES - 1)
    y = lax.axis_index("case") + turn * ((target >> 7) + first)
    hit = source == ((y * HALF + (lane & (HALF - 1))) & (combos - 1))
    return one_hot(hit & (lane < HALF)), one_hot(hit & (lane >= HALF))


def weights(comb, picked):
    return jnp.concatenate([dot(comb, p).astype(BF) for p in picked], axis=0)


def product(press, weight):
    half = press.shape[0] // 2
    return dot(jnp.concatenate([press[:half], press[half:]], axis=1), weight)


def case_rows(cases):
    return pl.ds(pl.multiple_of(lax.axis_index("case") * cases, cases), cases)


def project_kernel(press_hbm, comb_hbm, *refs):
    send_refs, (press_ref, comb_ref, sems) = refs[: NY - 1], refs[NY - 1 :]
    comb_copy = pltpu.make_async_copy(
        comb_hbm.at[case_rows(press_ref.shape[1])], comb_ref, sems.at[FETCHES]
    )
    comb_copy.start()
    part = press_ref.shape[0] // FETCHES
    copies = [
        pltpu.make_async_copy(
            press_hbm.at[pl.ds(i * part, part)], press_ref.at[pl.ds(i * part, part)], sems.at[i]
        )
        for i in range(FETCHES)
    ]
    for copy in copies:
        copy.start()
    picked = pieces(1, NY - 1, comb_ref.shape[1])
    comb_copy.wait()
    weight = weights(comb_ref[...], picked)
    for copy in copies:
        copy.wait()
    sent = product(press_ref[...], weight)
    for k, ref in enumerate(send_refs):
        ref[...] = sent[:, k * LANES : (k + 1) * LANES].astype(BF)


def rank_kernel(owner_ref, slot_ref, press_ref, comb_ref, place_ref, masks_ref, meta_ref, own_ref):
    panels = owner_ref.shape[1]
    me = lax.axis_index("se")
    owner = owner_ref[...]
    side = (owner ^ me) & 1
    chip = place_of(owner >> 1, owner & 1)
    owners = CHIPS * NC
    oh = jnp.where(iota((owners, panels), 0) == side * CHIPS + chip, 1.0, 0.0)
    width = 256
    ohs = [oh[:, b * width : (b + 1) * width] for b in range(panels // width)]
    before = one_hot(iota((width, width), 0) < iota((width, width), 1))
    counts = dot(jnp.concatenate(ohs, axis=0).astype(BF), before)
    start, ranks = jnp.zeros((owners, 1), F32), []
    for b, piece in enumerate(ohs):
        count = counts[b * owners : (b + 1) * owners]
        ranks.append(jnp.sum(piece * (count + start), axis=0, keepdims=True))
        start = start + count[:, width - 1 :] + piece[:, width - 1 :]
    rank = jnp.concatenate(ranks, axis=1).astype(jnp.int32)
    low, high = rank & (PER - 1), rank // PER
    place_ref[...] = one_hot(iota((GROUP * PER, panels), 0) == (chip & (GROUP - 1)) * PER + low)
    lanes = high * HALF + side * PER + low
    meta_ref[...] = lax.dot_general(
        (oh * (slot_ref[...] - 256).astype(F32)).astype(BF),
        one_hot(iota((LANES, panels), 0) == lanes),
        (((1,), (1,)), ((), ())),
        preferred_element_type=F32,
    ).astype(BF)
    group = side * 4 + (chip // GROUP) * 2 + high
    groups = jnp.transpose(jnp.broadcast_to(group.astype(F32), (LANES, panels)))
    part = (iota((1, LANES), 1) // HALF).astype(F32)
    for s in range(NC):
        for h in range(2):
            masks_ref[s, :, h * LANES : (h + 1) * LANES] = one_hot(groups == part + (s * 4 + h * 2))
    comb = comb_ref[case_rows(press_ref.shape[1]), :]
    own_ref[...] = product(press_ref[...], weights(comb, pieces(0, 1, comb.shape[1])))


def place_rows(rows, place_ref, mask_ref, meta_ref, out_ref):
    lane = iota(rows.shape, 1)
    turned = pltpu.roll(rows, HALF, 1)
    first = jnp.where(lane < HALF, rows, turned).astype(BF)
    second = jnp.where(lane < HALF, turned, rows).astype(BF)
    each = jnp.concatenate([first, second], axis=0)
    placed = dot(place_ref[...], jnp.concatenate([each, each], axis=1) * mask_ref[0])
    size = GROUP * PER
    for h in range(2):
        out_ref[h * size : (h + 1) * size, :] = placed[:, h * LANES : (h + 1) * LANES].astype(BF)
    out_ref[2 * size :, :] = meta_ref[...]


def sum_and_pack(own_ref, r1_ref, r2_ref, r3_ref, place_ref, mask_ref, meta_ref, out_ref, rows_ref):
    rows = own_ref[...] + r1_ref[...].astype(F32) + r2_ref[...].astype(F32) + r3_ref[...].astype(F32)
    rows_ref[...] = rows
    place_rows(rows, place_ref, mask_ref, meta_ref, out_ref)


def pack_kernel(rows_ref, place_ref, mask_ref, meta_ref, out_ref):
    place_rows(rows_ref[...], place_ref, mask_ref, meta_ref, out_ref)


def pack(kernel, side, rows, place, masks, meta, out_shape):
    whole = [pl.BlockSpec(a.shape, lambda i: (0, 0)) for a in rows]
    return call(
        kernel,
        out_shape,
        (*rows, place, masks, meta),
        1 << 30,
        "pack",
        grid=(1,),
        in_specs=whole
        + [
            pl.BlockSpec(place.shape, lambda i: (0, 0)),
            pl.BlockSpec((1,) + masks.shape[1:], lambda i: (side, 0, 0)),
            pl.BlockSpec((CHIPS, LANES), lambda i: (side, 0)),
        ],
        out_specs=jax.tree.map(lambda s: pl.BlockSpec(s.shape, lambda i: (0, 0)), out_shape),
    )


def scatter_kernel(msg_ref, out_ref):
    points = 2 * out_ref.shape[0]
    point = (iota((points, LANES), 0) - 256).astype(F32).astype(BF)
    left = iota((1, LANES), 1) < HALF
    one, zero = jnp.ones((), BF), jnp.zeros((), BF)
    lows, highs, data = [], [], []
    for j in range(0, CHIPS, 2):
        a, b = (
            msg_ref[i, NC * PER :, :].astype(F32)[:1, :] for i in (j, j + 1)
        )
        low = jnp.where(left, a, pltpu.roll(b, HALF, 1)).astype(BF)
        high = jnp.where(left, pltpu.roll(a, HALF, 1), b).astype(BF)
        lows.append(jnp.where(point == low, one, zero))
        highs.append(jnp.where(point == high, one, zero))
        data += [msg_ref[i, : NC * PER, :] for i in (j, j + 1)]
    rows = jnp.concatenate(data, axis=0)
    total = dot(jnp.concatenate(lows, axis=1), rows)
    total = total + pltpu.roll(dot(jnp.concatenate(highs, axis=1), rows), HALF, 1)
    half = points // 2
    right = pltpu.roll(total[half:], HALF, 1)
    out_ref[...] = jnp.where(left, total[:half], right).astype(BF)


def finish_kernel(live_ref, *refs):
    loads, (mat_ref, out_ref, block_ref, sems) = refs[:NY], refs[NY:]
    y = lax.axis_index("case")
    rows, combos = block_ref.shape
    source, target = iota((NY * LANES, combos), 0), iota((NY * LANES, combos), 1)
    lane = source & (LANES - 1)
    turn = 1 - 2 * (lax.axis_index("se") & 1)
    hit = ((y - turn * (source >> 7)) & (NY - 1)) * HALF + (lane & (HALF - 1)) == target
    every = jnp.concatenate([ref[...] for ref in loads], axis=1)
    upper = dot(every, one_hot(hit & (lane < HALF)))
    lower = dot(every, one_hot(hit & (lane >= HALF)))
    total = jnp.concatenate([upper, lower], axis=0).astype(BF)
    part = rows // OUT_PARTS
    copies = []
    for p in range(OUT_PARTS):
        at = pl.ds(p * part, part)
        out = dot(mat_ref[at, :], total)
        live = y * rows + p * part + iota(out.shape, 0) < live_ref[0]
        block_ref[at, :] = jnp.where(live, out, 0.0).astype(BF)
        copies.append(pltpu.make_async_copy(block_ref.at[at], out_ref.at[at], sems.at[p]))
        copies[-1].start()
    for copy in copies:
        copy.wait()


def place_of(chip, core):
    return (chip * 5 - 12 * core) & (CHIPS - 1)


def chip_at(place, core):
    return ((place + 12 * core) * 13) & (CHIPS - 1)


SAME_CORE = [[chip_at(place, c) * NC + c for place in range(CHIPS)] for c in range(NC)]
OTHER_CORE = [(i, i ^ 1) for i in range(NX * NZ * NC)]


def along_y(a, k):
    owners = NX * NZ * NC
    pairs = [
        (y * owners + i, (y + (k if i % NC == 0 else -k)) % NY * owners + i)
        for y in range(NY)
        for i in range(owners)
    ]
    return lax.ppermute(a, ("case", "se"), pairs)


def shape(*dims, dtype=BF):
    return jax.ShapeDtypeStruct(dims, dtype)


def per_device(
    panel_press, panel_owner, panel_slot, elem_count, flexibility, stress_matrix, combination
):
    panels = panel_press.shape[0]
    points, combos = flexibility.shape[2], combination.shape[1]
    half = panels // 2
    sent = call(
        project_kernel,
        [shape(half, LANES)] * (NY - 1),
        (panel_press, combination),
        1 << 28,
        "project",
        in_specs=[pl.BlockSpec(memory_space=pltpu.HBM)] * 2,
        vmem=FETCH_VMEM,
        scratch_shapes=[
            pltpu.VMEM(panel_press.shape, BF),
            pltpu.VMEM((panel_press.shape[1], combos), BF),
            pltpu.SemaphoreType.DMA((FETCHES + 1,)),
        ],
    )
    parts = [along_y(sent[k - 1], k) for k in range(1, NY)]
    place, masks, meta, own = call(
        rank_kernel,
        (
            shape(GROUP * PER, panels),
            shape(NC, panels, 2 * LANES),
            shape(NC * CHIPS, LANES),
            shape(half, LANES, dtype=F32),
        ),
        (panel_owner.reshape(1, panels), panel_slot.reshape(1, panels), panel_press, combination),
        1 << 28,
        "rank",
    )
    mat = dot(stress_matrix[0], flexibility[0]).astype(BF)
    parts, mat = lax.optimization_barrier((parts, mat))
    packed = shape(CHIPS * PER + CHIPS, LANES)
    theirs, rows = pack(
        sum_and_pack, 1, [own, *parts], place, masks, meta, (packed, shape(half, LANES, dtype=F32))
    )
    theirs = lax.ppermute(theirs, "se", OTHER_CORE)
    ours = pack(pack_kernel, 0, [rows], place, masks, meta, packed)
    slots = ours[CHIPS * PER :] + theirs[CHIPS * PER :]
    messages = jnp.concatenate(
        [
            ours[: CHIPS * PER].reshape(CHIPS, PER, LANES),
            theirs[: CHIPS * PER].reshape(CHIPS, PER, LANES),
            jnp.broadcast_to(slots[:, None, :], (CHIPS, MSG - NC * PER, LANES)),
        ],
        axis=1,
    )
    messages = lax.all_to_all(messages, "se", 0, 0, axis_index_groups=SAME_CORE, tiled=True)
    loads = [call(scatter_kernel, shape(points // 2, LANES), (messages,), 1 << 30, "scatter")]
    loads += [along_y(loads[0], k) for k in range(1, NY)]
    local = mat.shape[0]
    vmem = pl.BlockSpec(memory_space=pltpu.VMEM)
    out = call(
        finish_kernel,
        shape(local, combos),
        (elem_count, *loads, mat),
        1 << 28,
        "finish",
        in_specs=[pl.BlockSpec(memory_space=pltpu.SMEM)] + [vmem] * (NY + 1),
        out_specs=pl.BlockSpec(memory_space=pltpu.HBM),
        scratch_shapes=[pltpu.VMEM((local, combos), BF), pltpu.SemaphoreType.DMA((OUT_PARTS,))],
    )
    return out[None]


def solution(mesh):
    return jax.shard_map(
        per_device,
        mesh=mesh,
        in_specs=(
            P("se", "case"),
            P("se", None),
            P("se"),
            P("se"),
            P("se", None, None),
            P("se", "case", None),
            P(),
        ),
        out_specs=P("se", "case", None),
        check_vma=False,
    )
```

```python
import jax
import jax.numpy as jnp
from jax import lax
from jax.experimental import pallas as pl
from jax.experimental.pallas import tpu as pltpu
from jax.sharding import PartitionSpec as P

NX, NZ, NC, NY = 4, 8, 2, 4
CAP = 64
CHIPS = NX * NZ
LANES, HALF = 128, 64
PER = CAP // 2
GROUP = 16
MSG = NC * PER + 8
OUT_PARTS = 4
FETCHES = 8
FETCH_VMEM = 53
BF, F32 = jnp.bfloat16, jnp.float32


def iota(shape, dim):
    return lax.broadcasted_iota(jnp.int32, shape, dim)


def one_hot(mask):
    return jnp.where(mask, 1.0, 0.0).astype(BF)


def dot(a, b):
    return jnp.dot(a, b, preferred_element_type=F32)


def call(kernel, out_shape, args, flops, name, in_specs=None, vmem=32, **more):
    if in_specs is not None:
        more["in_specs"] = in_specs
    return pl.pallas_call(
        kernel,
        out_shape=out_shape,
        compiler_params=pltpu.CompilerParams(vmem_limit_bytes=vmem << 20),
        cost_estimate=pl.CostEstimate(flops=flops, bytes_accessed=2 << 20, transcendentals=0),
        name=name,
        **more,
    )(*args)


def pieces(first, count, combos):
    turn = 1 - 2 * (lax.axis_index("se") & 1)
    source, target = iota((combos, count * LANES), 0), iota((combos, count * LANES), 1)
    lane = target & (LANES - 1)
    y = lax.axis_index("case") + turn * ((target >> 7) + first)
    hit = source == ((y * HALF + (lane & (HALF - 1))) & (combos - 1))
    return one_hot(hit & (lane < HALF)), one_hot(hit & (lane >= HALF))


def weights(comb, picked):
    return jnp.concatenate([dot(comb, p).astype(BF) for p in picked], axis=0)


def product(press, weight):
    half = press.shape[0] // 2
    return dot(jnp.concatenate([press[:half], press[half:]], axis=1), weight)


def case_rows(cases):
    return pl.ds(pl.multiple_of(lax.axis_index("case") * cases, cases), cases)


def project_kernel(press_hbm, comb_hbm, *refs):
    send_refs, (press_ref, comb_ref, sems) = refs[: NY - 1], refs[NY - 1 :]
    comb_copy = pltpu.make_async_copy(
        comb_hbm.at[case_rows(press_ref.shape[1])], comb_ref, sems.at[FETCHES]
    )
    comb_copy.start()
    part = press_ref.shape[0] // FETCHES
    copies = [
        pltpu.make_async_copy(
            press_hbm.at[pl.ds(i * part, part)], press_ref.at[pl.ds(i * part, part)], sems.at[i]
        )
        for i in range(FETCHES)
    ]
    for copy in copies:
        copy.start()
    picked = pieces(1, NY - 1, comb_ref.shape[1])
    comb_copy.wait()
    weight = weights(comb_ref[...], picked)
    for copy in copies:
        copy.wait()
    sent = product(press_ref[...], weight)
    for k, ref in enumerate(send_refs):
        ref[...] = sent[:, k * LANES : (k + 1) * LANES].astype(BF)


def rank_kernel(owner_ref, slot_ref, press_ref, comb_ref, place_ref, masks_ref, meta_ref, own_ref):
    panels = owner_ref.shape[1]
    me = lax.axis_index("se")
    owner = owner_ref[...]
    side = (owner ^ me) & 1
    chip = place_of(owner >> 1, owner & 1)
    owners = CHIPS * NC
    oh = jnp.where(iota((owners, panels), 0) == side * CHIPS + chip, 1.0, 0.0)
    width = 256
    ohs = [oh[:, b * width : (b + 1) * width] for b in range(panels // width)]
    before = one_hot(iota((width, width), 0) < iota((width, width), 1))
    counts = dot(jnp.concatenate(ohs, axis=0).astype(BF), before)
    start, ranks = jnp.zeros((owners, 1), F32), []
    for b, piece in enumerate(ohs):
        count = counts[b * owners : (b + 1) * owners]
        ranks.append(jnp.sum(piece * (count + start), axis=0, keepdims=True))
        start = start + count[:, width - 1 :] + piece[:, width - 1 :]
    rank = jnp.concatenate(ranks, axis=1).astype(jnp.int32)
    low, high = rank & (PER - 1), rank // PER
    place_ref[...] = one_hot(iota((GROUP * PER, panels), 0) == (chip & (GROUP - 1)) * PER + low)
    lanes = high * HALF + side * PER + low
    meta_ref[...] = lax.dot_general(
        (oh * (slot_ref[...] - 256).astype(F32)).astype(BF),
        one_hot(iota((LANES, panels), 0) == lanes),
        (((1,), (1,)), ((), ())),
        preferred_element_type=F32,
    ).astype(BF)
    group = side * 4 + (chip // GROUP) * 2 + high
    groups = jnp.transpose(jnp.broadcast_to(group.astype(F32), (LANES, panels)))
    part = (iota((1, LANES), 1) // HALF).astype(F32)
    for s in range(NC):
        for h in range(2):
            masks_ref[s, :, h * LANES : (h + 1) * LANES] = one_hot(groups == part + (s * 4 + h * 2))
    comb = comb_ref[case_rows(press_ref.shape[1]), :]
    own_ref[...] = product(press_ref[...], weights(comb, pieces(0, 1, comb.shape[1])))


def place_rows(rows, place_ref, mask_ref, meta_ref, out_ref):
    lane = iota(rows.shape, 1)
    turned = pltpu.roll(rows, HALF, 1)
    first = jnp.where(lane < HALF, rows, turned).astype(BF)
    second = jnp.where(lane < HALF, turned, rows).astype(BF)
    each = jnp.concatenate([first, second], axis=0)
    placed = dot(place_ref[...], jnp.concatenate([each, each], axis=1) * mask_ref[0])
    size = GROUP * PER
    for h in range(2):
        out_ref[h * size : (h + 1) * size, :] = placed[:, h * LANES : (h + 1) * LANES].astype(BF)
    out_ref[2 * size :, :] = meta_ref[...]


def sum_and_pack(own_ref, r1_ref, r2_ref, r3_ref, place_ref, mask_ref, meta_ref, out_ref, rows_ref):
    rows = own_ref[...] + r1_ref[...].astype(F32) + r2_ref[...].astype(F32) + r3_ref[...].astype(F32)
    rows_ref[...] = rows
    place_rows(rows, place_ref, mask_ref, meta_ref, out_ref)


def pack_kernel(rows_ref, place_ref, mask_ref, meta_ref, out_ref):
    place_rows(rows_ref[...], place_ref, mask_ref, meta_ref, out_ref)


def pack(kernel, side, rows, place, masks, meta, out_shape):
    whole = [pl.BlockSpec(a.shape, lambda i: (0, 0)) for a in rows]
    return call(
        kernel,
        out_shape,
        (*rows, place, masks, meta),
        1 << 30,
        "pack",
        grid=(1,),
        in_specs=whole
        + [
            pl.BlockSpec(place.shape, lambda i: (0, 0)),
            pl.BlockSpec((1,) + masks.shape[1:], lambda i: (side, 0, 0)),
            pl.BlockSpec((CHIPS, LANES), lambda i: (side, 0)),
        ],
        out_specs=jax.tree.map(lambda s: pl.BlockSpec(s.shape, lambda i: (0, 0)), out_shape),
    )


def scatter_kernel(msg_ref, out_ref):
    points = 2 * out_ref.shape[0]
    point = (iota((points, LANES), 0) - 256).astype(F32).astype(BF)
    left = iota((1, LANES), 1) < HALF
    one, zero = jnp.ones((), BF), jnp.zeros((), BF)
    lows, highs, data = [], [], []
    for j in range(0, CHIPS, 2):
        a, b = (
            msg_ref[i, NC * PER :, :].astype(F32)[:1, :] for i in (j, j + 1)
        )
        low = jnp.where(left, a, pltpu.roll(b, HALF, 1)).astype(BF)
        high = jnp.where(left, pltpu.roll(a, HALF, 1), b).astype(BF)
        lows.append(jnp.where(point == low, one, zero))
        highs.append(jnp.where(point == high, one, zero))
        data += [msg_ref[i, : NC * PER, :] for i in (j, j + 1)]
    rows = jnp.concatenate(data, axis=0)
    total = dot(jnp.concatenate(lows, axis=1), rows)
    total = total + pltpu.roll(dot(jnp.concatenate(highs, axis=1), rows), HALF, 1)
    half = points // 2
    right = pltpu.roll(total[half:], HALF, 1)
    out_ref[...] = jnp.where(left, total[:half], right).astype(BF)


def finish_kernel(live_ref, *refs):
    loads, (mat_ref, out_ref, block_ref, sems) = refs[:NY], refs[NY:]
    y = lax.axis_index("case")
    rows, combos = block_ref.shape
    source, target = iota((NY * LANES, combos), 0), iota((NY * LANES, combos), 1)
    lane = source & (LANES - 1)
    turn = 1 - 2 * (lax.axis_index("se") & 1)
    hit = ((y - turn * (source >> 7)) & (NY - 1)) * HALF + (lane & (HALF - 1)) == target
    every = jnp.concatenate([ref[...] for ref in loads], axis=1)
    upper = dot(every, one_hot(hit & (lane < HALF)))
    lower = dot(every, one_hot(hit & (lane >= HALF)))
    total = jnp.concatenate([upper, lower], axis=0).astype(BF)
    part = rows // OUT_PARTS
    copies = []
    for p in range(OUT_PARTS):
        at = pl.ds(p * part, part)
        out = dot(mat_ref[at, :], total)
        live = y * rows + p * part + iota(out.shape, 0) < live_ref[0]
        block_ref[at, :] = jnp.where(live, out, 0.0).astype(BF)
        copies.append(pltpu.make_async_copy(block_ref.at[at], out_ref.at[at], sems.at[p]))
        copies[-1].start()
    for copy in copies:
        copy.wait()


def place_of(chip, core):
    return (((chip & 7) * 4 + (chip >> 3)) * 13 - 12 * core) & (CHIPS - 1)


SAME_CORE = [
    [chip * NC + c for chip in sorted(range(CHIPS), key=lambda chip: place_of(chip, c))] for c in range(NC)
]
OTHER_CORE = [(i, i ^ 1) for i in range(NX * NZ * NC)]


def along_y(a, k):
    owners = NX * NZ * NC
    pairs = [
        (y * owners + i, (y + (k if i % NC == 0 else -k)) % NY * owners + i)
        for y in range(NY)
        for i in range(owners)
    ]
    return lax.ppermute(a, ("case", "se"), pairs)


def shape(*dims, dtype=BF):
    return jax.ShapeDtypeStruct(dims, dtype)


def per_device(
    panel_press, panel_owner, panel_slot, elem_count, flexibility, stress_matrix, combination
):
    panels = panel_press.shape[0]
    points, combos = flexibility.shape[2], combination.shape[1]
    half = panels // 2
    sent = call(
        project_kernel,
        [shape(half, LANES)] * (NY - 1),
        (panel_press, combination),
        1 << 28,
        "project",
        in_specs=[pl.BlockSpec(memory_space=pltpu.HBM)] * 2,
        vmem=FETCH_VMEM,
        scratch_shapes=[
            pltpu.VMEM(panel_press.shape, BF),
            pltpu.VMEM((panel_press.shape[1], combos), BF),
            pltpu.SemaphoreType.DMA((FETCHES + 1,)),
        ],
    )
    parts = [along_y(sent[k - 1], k) for k in range(1, NY)]
    place, masks, meta, own = call(
        rank_kernel,
        (
            shape(GROUP * PER, panels),
            shape(NC, panels, 2 * LANES),
            shape(NC * CHIPS, LANES),
            shape(half, LANES, dtype=F32),
        ),
        (panel_owner.reshape(1, panels), panel_slot.reshape(1, panels), panel_press, combination),
        1 << 28,
        "rank",
    )
    mat = dot(stress_matrix[0], flexibility[0]).astype(BF)
    parts, mat = lax.optimization_barrier((parts, mat))
    packed = shape(CHIPS * PER + CHIPS, LANES)
    theirs, rows = pack(
        sum_and_pack, 1, [own, *parts], place, masks, meta, (packed, shape(half, LANES, dtype=F32))
    )
    theirs = lax.ppermute(theirs, "se", OTHER_CORE)
    ours = pack(pack_kernel, 0, [rows], place, masks, meta, packed)
    slots = ours[CHIPS * PER :] + theirs[CHIPS * PER :]
    messages = jnp.concatenate(
        [
            ours[: CHIPS * PER].reshape(CHIPS, PER, LANES),
            theirs[: CHIPS * PER].reshape(CHIPS, PER, LANES),
            jnp.broadcast_to(slots[:, None, :], (CHIPS, MSG - NC * PER, LANES)),
        ],
        axis=1,
    )
    messages = lax.all_to_all(messages, "se", 0, 0, axis_index_groups=SAME_CORE, tiled=True)
    loads = [call(scatter_kernel, shape(points // 2, LANES), (messages,), 1 << 30, "scatter")]
    loads += [along_y(loads[0], k) for k in range(1, NY)]
    local = mat.shape[0]
    vmem = pl.BlockSpec(memory_space=pltpu.VMEM)
    out = call(
        finish_kernel,
        shape(local, combos),
        (elem_count, *loads, mat),
        1 << 28,
        "finish",
        in_specs=[pl.BlockSpec(memory_space=pltpu.SMEM)] + [vmem] * (NY + 1),
        out_specs=pl.BlockSpec(memory_space=pltpu.HBM),
        scratch_shapes=[pltpu.VMEM((local, combos), BF), pltpu.SemaphoreType.DMA((OUT_PARTS,))],
    )
    return out[None]


def solution(mesh):
    return jax.shard_map(
        per_device,
        mesh=mesh,
        in_specs=(
            P("se", "case"),
            P("se", None),
            P("se"),
            P("se"),
            P("se", None, None),
            P("se", "case", None),
            P(),
        ),
        out_specs=P("se", "case", None),
        check_vma=False,
    )
```
